32 devices in a mesh: grp: 2 (over x), gx: 16 (over z, y, core).
Axes of the slice: x: 2, y: 2, z: 4, core: 2. Of those that a mesh axis runs over, the one named last changes fastest.
Arguments:
- state_field: float32 [32, 20, 16, 512], P(('grp', 'gx')), parts along dimension 0, may hold values from -6 to 6
- cotangent: float32 [32, 20, 16, 512], P(('grp', 'gx')), parts along dimension 0, may hold values from -6 to 6
- spec_weight: float32 [192, 12, 12, 2, 20, 20], P('gx'), may hold values from -2.5 to 2.5
- point_weight: float32 [20, 20], replicated, may hold values from -1.25 to 1.25
- bias_vector: float32 [20], replicated, may hold values from -3 to 3
Outputs:
- layer_out: float32 [32, 20, 16, 512], P(('grp', 'gx')), parts along dimension 0
- field_grad: float32 [32, 20, 16, 512], P(('grp', 'gx')), parts along dimension 0
- spec_grad: float32 [384, 12, 12, 2, 20, 20], P(('grp', 'gx')), parts along dimension 0
- point_grad: float32 [40, 20], P('grp'), parts along dimension 0
- bias_grad: float32 [40], P('grp'), parts along dimension 0
The draws below stay inside these ranges and needn't reach their ends.
There are 2 independent parts, one for each index of `grp`. The reference program is written for one: setup_inputs(seed, part) draws one part's arguments, and reference() takes and returns one part's arrays. A program takes and returns all parts, laid end to end along the dimension named above; an argument that names none is the same for every part. Nothing has to cross between parts.
All inputs are finite; a program needn't handle non-finite values.
Results may differ from the reference program's by a relative error of at most 0.00011.
Values sent between devices are 32-bit elements; how exact they have to be, the bound alone decides.
A program may use at most 320 MiB of HBM per device.

```python
import jax
import jax.numpy as jnp
import numpy as np
from jax import lax

C = 20
MX = 12
MY = 12
MZ = 24
MT = 8
NY = 16
NZ = 32
NT = 16
NX = 16
ZT = 512
MZT = 192


def levels(stream_key, shape, shards, smallest, high):
    def one(axis_at, shards_of):
        steps = jax.random.uniform(jax.random.fold_in(jax.random.fold_in(stream_key, 6), axis_at), (shards_of,), jnp.float32, smallest / len(shards), high / len(shards))
        return jnp.repeat(jnp.exp(steps), shape[axis_at] // shards_of).reshape((-1,) + (1,) * (len(shape) - axis_at - 1))

    loudness = one(*shards[0])
    for cut in shards[1:]:
        loudness = loudness * one(*cut)
    return loudness


def centred(rng, shape, scale, limit, shards=(), kind=jnp.bfloat16):
    entries = jax.random.normal(rng, shape, jnp.float32) * scale
    if len(shards) > 0:
        entries = levels(rng, shape, shards, -0.22, 0.18) * entries
    return jnp.clip(entries, min=-limit, max=limit).astype(kind)


def setup_inputs(seed: int = 0, part: int = 0) -> dict:
    splits = jax.random.split(jax.random.key(seed), 6)
    part_keys = jax.random.split(jax.random.fold_in(splits[5], part), 6)
    state_field = centred(part_keys[0], (NX, C, NY, ZT), 1.0, 6.0, ((0, 16),), jnp.float32)
    cotangent = centred(part_keys[1], (NX, C, NY, ZT), 1.0, 6.0, ((0, 16),), jnp.float32)
    spec_weight = centred(splits[2], (MZT, MY, MX, 2, C, C), (C // 4) ** -0.5, 2.5, ((0, 16),), jnp.float32)
    point_weight = centred(splits[3], (C, C), C ** -0.5, 1.25, (), jnp.float32)
    bias_vector = centred(splits[4], (C,), 0.5, 3.0, (), jnp.float32)
    return dict(state_field=state_field, cotangent=cotangent, spec_weight=spec_weight, point_weight=point_weight, bias_vector=bias_vector)


def kept_index(count, length):
    return np.concatenate([np.arange(count // 2), np.arange(length - count // 2, length)])

def forward(state_field, spec_weight, point_weight, bias_vector):
    index_x = kept_index(MX, NX)
    index_y = kept_index(MY, NY)
    index_z = kept_index(MZ, NZ)
    grid_five = state_field.reshape(NX, C, NY, NZ, NT)
    whole = jnp.fft.rfftn(grid_five, axes=(0, 2, 3, 4), norm='ortho')
    spectrum = whole[index_x][:, :, index_y][:, :, :, index_z][..., :MT]
    shaped = spec_weight.reshape(MZ, MT, MY, MX, 2, C, C)
    complex_weight = shaped[..., 0, :, :] + 1j * shaped[..., 1, :, :]
    mixed = jnp.einsum('ztyxio,xiyzt->xoyzt', complex_weight, spectrum)
    step_one = jnp.zeros((NX, C, MY, MZ, MT), mixed.dtype).at[index_x].set(mixed)
    step_two = jnp.zeros((NX, C, NY, MZ, MT), mixed.dtype).at[:, :, index_y].set(step_one)
    step_three = jnp.zeros((NX, C, NY, NZ, MT), mixed.dtype).at[:, :, :, index_z].set(step_two)
    padded = jnp.pad(step_three, ((0, 0), (0, 0), (0, 0), (0, 0), (0, NT // 2 + 1 - MT)))
    spectral = jnp.fft.irfftn(padded, s=(NX, NY, NZ, NT), axes=(0, 2, 3, 4), norm='ortho')
    spectral = spectral.reshape(NX, C, NY, NZ * NT)
    local_part = jnp.einsum('xiyn,io->xoyn', state_field, point_weight, precision=lax.Precision.HIGHEST)
    pre = spectral + local_part + bias_vector[None, :, None, None]
    return jax.nn.gelu(pre, approximate=False)

def reference(state_field, cotangent, spec_weight, point_weight, bias_vector):
    layer_out, pullback = jax.vjp(forward, state_field, spec_weight, point_weight, bias_vector)
    field_grad, spec_grad, point_raw, bias_raw = pullback(cotangent)
    norm_scale = float(NX * NY * NZ * NT) ** (-0.5)
    return (layer_out, field_grad, spec_grad, point_raw * norm_scale, bias_raw * norm_scale)
```

```python
import functools
import math

import jax
import jax.numpy as jnp
import numpy as np
from jax import lax
from jax.experimental import pallas as pl
from jax.experimental.pallas import tpu as pltpu
from jax.sharding import PartitionSpec as P

C = 20
MX = 12
MY = 12
MZ = 24
MT = 8
NZ = 32
NT = 16
NY = 16
ZT = NZ * NT
MZT = MZ * MT
CY = C * NY
HALF = MY // 2
LANES = 256
BF = jnp.bfloat16
F32 = jnp.float32
NN = ((1,), (0,))
NT_DIMS = ((1,), (1,))


def column(ky):
    return (ky // HALF) * 128 + (ky % HALF) * C


def freqs(count):
    modes = np.arange(count)
    return np.where(modes < count // 2, modes, modes - count)


def angles(count, length):
    phase = np.mod(freqs(count)[:, None] * np.arange(length)[None, :], length)
    return 2.0 * np.pi / length * phase


def halves(table):
    table = np.asarray(table, np.float64)
    high = table.astype(jnp.bfloat16)
    low = (table - high.astype(np.float64)).astype(jnp.bfloat16)
    return np.stack([high, low])


def depth_time(full_x, owners, doubled):
    scale = float(full_x * NY * ZT) ** (-0.5)
    modes = np.arange(MZT)
    depth = freqs(MZ)[modes // MT]
    time = modes % MT
    cells = np.arange(ZT)
    phase = depth[:, None] * (cells // NT)[None, :] * NT + time[:, None] * (cells % NT)[None, :] * NZ
    angle = 2.0 * np.pi / ZT * np.mod(phase, ZT)
    factor = np.full((MZT, 1), scale)
    if doubled:
        factor = factor * np.where(time == 0, 1.0, 2.0)[:, None]
    real, imag = factor * np.cos(angle), -factor * np.sin(angle)

    def rows(first, second):
        both = np.stack([first, second]).reshape(2, owners, MZT // owners, ZT)
        return both.transpose(1, 0, 2, 3).reshape(2 * MZT, ZT)

    return halves(np.stack([rows(real, imag), rows(imag, -real)]))


def y_tables():
    angle = angles(MY, NY)
    out = np.zeros((2, C, NY, LANES))
    for ky in range(MY):
        for c in range(C):
            out[0, c, :, column(ky) + c] = np.cos(angle[ky])
            out[1, c, :, column(ky) + c] = np.sin(angle[ky])
    return halves(out.reshape(2, CY, LANES))


def x_tables(full_x, owned):
    angle = angles(MX, full_x)
    cos, sin = np.cos(angle), np.sin(angle)
    eye = np.eye(owned)
    to_real = np.stack([cos, sin])
    to_imag = np.stack([-sin, cos])

    def lift(pair):
        grown = np.einsum("tpkx,mn->xpmntk", pair, eye)
        return grown.reshape(full_x * 2 * owned, owned * 2 * MX)

    even = lift(np.stack([to_real, to_imag]))
    odd = lift(np.stack([-to_imag, to_real]))
    modes = even.T
    from_real = np.stack([cos, sin])
    from_imag = np.stack([-sin, cos])
    lower = lift(np.stack([from_real, from_imag]))
    lower_odd = lift(np.stack([-from_imag, from_real]))
    return halves(np.stack([even, odd])), halves(modes), halves(np.stack([lower, lower_odd]))


def small_tables():
    place = np.zeros((2, C, NY, LANES))
    for i in range(C):
        j = i % 16
        place[i // 16, i, :, (j // 8) * 128 + 120 + j % 8] = 1.0
    spot = np.zeros((2, 2 * MZT, C, NY))
    for o in range(C):
        spot[0, 2 * o, o] = 1.0
        spot[1, 2 * o + 1, o] = 1.0
    return (
        place.reshape(2, CY, LANES).astype(jnp.bfloat16),
        spot.reshape(2, 2 * MZT, CY).astype(jnp.bfloat16),
    )


def split(value):
    high = value.astype(BF)
    return high, (value - high.astype(F32)).astype(BF)


def product(left, right, dims):
    def one(a, b):
        return lax.dot_general(a, b, (dims, ((), ())), preferred_element_type=F32)

    return one(left[0], right[0]) + (one(left[0], right[1]) + one(left[1], right[0]))


def table(ref, *index):
    return ref[(0,) + index], ref[(1,) + index]


def to_rows(field, depth_ref, y_ref):
    out = None
    for k in range(2):
        lifted = product(table(depth_ref, k), field, NT_DIMS)
        term = product(split(lifted), table(y_ref, k), NN)
        out = term if out is None else out + term
    return out


def to_cells(rows, depth_ref, y_ref):
    out = None
    for k in range(2):
        spread = product(table(y_ref, k), rows, NT_DIMS)
        term = product(split(spread), table(depth_ref, k), NN)
        out = term if out is None else out + term
    return out


def lift_kernel(field_ref, depth_ref, y_ref, out_ref):
    out_ref[...] = to_rows(split(field_ref[...]), depth_ref, y_ref)


def middle_kernel(
    rows_ref, field_ref, cot_ref, mix_ref, bias_ref, depth_ref, y_ref, place_ref, spot_ref,
    out_ref, dpre_ref, send_ref,
):
    field = split(field_ref[...])
    pre = to_cells(split(rows_ref[...]), depth_ref, y_ref)
    pre = pre + product(split(mix_ref[...]), field, NN) + bias_ref[...]
    cumulative = 0.5 * (1.0 + lax.erf(pre * (1.0 / math.sqrt(2.0))))
    density = jnp.exp(-0.5 * pre * pre) * (1.0 / math.sqrt(2.0 * math.pi))
    out_ref[...] = pre * cumulative
    dpre = cot_ref[...] * (cumulative + pre * density)
    dpre_ref[...] = dpre
    parts = split(dpre)
    send = to_rows(parts, depth_ref, y_ref)
    cross = product(parts, field, NT_DIMS)
    row = lax.broadcasted_iota(jnp.int32, (CY, CY), 0)
    col = lax.broadcasted_iota(jnp.int32, (CY, CY), 1)
    cross = split(jnp.where((row % NY) == (col % NY), cross, 0.0))
    lane = lax.broadcasted_iota(jnp.int32, (CY, LANES), 1)
    total = jnp.sum(dpre, axis=1, keepdims=True)
    for k in range(2):
        moved = jnp.dot(cross[0], place_ref[k], preferred_element_type=F32)
        moved = moved + jnp.dot(cross[1], place_ref[k], preferred_element_type=F32)
        if k == 1:
            moved = moved + jnp.where(lane == 124, total, 0.0)
        high, low = split(moved)
        send = send + jnp.dot(spot_ref[k], high, preferred_element_type=F32)
        send = send + jnp.dot(spot_ref[k], low, preferred_element_type=F32)
    send_ref[...] = send


def last_kernel(rows_ref, dpre_ref, mix_ref, depth_ref, y_ref, out_ref):
    grad = to_cells(split(rows_ref[...]), depth_ref, y_ref)
    out_ref[...] = grad + product(split(mix_ref[...]), split(dpre_ref[...]), NN)


def gather_kernel(owned, rows_ref, x_ref, ab_ref, even_ref, odd_ref):
    turned = split(rows_ref[...].T)
    even_ref[...] = product(turned, table(x_ref, 0), NN)
    odd_ref[...] = product(turned, table(x_ref, 1), NN)
    for m in range(owned):
        for p, ref in enumerate((even_ref, odd_ref)):
            part = ref[:, m * 24:(m + 1) * 24]
            part = jnp.concatenate([part, jnp.zeros((LANES, 104), F32)], axis=1)
            for ky in range(MY):
                ab_ref[m, pl.ds(ky * 40 + p, C, stride=2), :] = part[column(ky):column(ky) + C]


def mix_kernel(weight_ref, ab_ref, out_ref):
    def body(ky, carry):
        ab = ab_ref[0, pl.ds(pl.multiple_of(ky * 40, 8), 40), :]
        for kx in range(MX):
            start = pl.multiple_of(ky * 480 + kx * 40, 8)
            weight = weight_ref[pl.ds(start, 40), :]
            for p in range(2):
                lane = p * MX + kx
                out = jnp.sum(weight * ab[:, lane:lane + 1], axis=0, keepdims=True)
                out_ref[0, ky, lane:lane + 1, :] = out
        return carry

    lax.fori_loop(0, MY, body, 0)


def spread_kernel(owned, modes_ref, x_ref, out_ref, full_ref):
    full_ref[...] = jnp.zeros_like(full_ref)
    for ky in range(MY):
        part = modes_ref[:, ky].reshape(owned * 24, C)
        full_ref[:, column(ky):column(ky) + C] = part
    out_ref[...] = product(table(x_ref, 0), split(full_ref[...]), NN)


def back_modes_kernel(owned, rows_ref, x_ref, out_ref):
    modes = product(table(x_ref), split(rows_ref[...]), NN)
    for ky in range(MY):
        part = modes[:, column(ky):column(ky) + C]
        out_ref[:, ky] = part.reshape(owned, 24, C)


def grad_kernel(weight_ref, ab_ref, back_ref, grad_ref, sums_ref):
    lanes = lax.broadcasted_iota(jnp.int32, (40, 128), 1)

    def body(ky, carry):
        rows = pl.ds(pl.multiple_of(ky * 40, 8), 40)
        ab = ab_ref[0, rows, :]
        back = back_ref[0, ky]
        sums = jnp.zeros((40, 128), F32)
        for kx in range(MX):
            start = pl.multiple_of(ky * 480 + kx * 40, 8)
            weight = weight_ref[pl.ds(start, 40), :]
            real = back[kx:kx + 1, :]
            imag = back[MX + kx:MX + kx + 1, :]
            grad_ref[pl.ds(start, 40), :] = (
                ab[:, kx:kx + 1] * real + ab[:, MX + kx:MX + kx + 1] * imag
            )
            first = jnp.sum(weight * real, axis=1, keepdims=True)
            second = jnp.sum(weight * imag, axis=1, keepdims=True)
            sums = jnp.where(lanes == kx, first, sums)
            sums = jnp.where(lanes == MX + kx, second, sums)
        sums_ref[0, rows, :] = sums
        return carry

    lax.fori_loop(0, MY, body, 0)


def back_spread_kernel(owned, sums_ref, x_ref, rows_ref, out_ref, even_ref, odd_ref):
    even_ref[...] = jnp.zeros_like(even_ref)
    odd_ref[...] = jnp.zeros_like(odd_ref)
    for m in range(owned):
        for p, ref in enumerate((even_ref, odd_ref)):
            for ky in range(MY):
                part = sums_ref[m, pl.ds(ky * 40 + p, C, stride=2), :]
                ref[column(ky):column(ky) + C, m * 24:(m + 1) * 24] = part[:, :24]
    out = product(table(x_ref, 0), split(even_ref[...]), NT_DIMS)
    out = out + product(table(x_ref, 1), split(odd_ref[...]), NT_DIMS)
    peers, each, _ = rows_ref.shape
    lane = lax.broadcasted_iota(jnp.int32, (each, LANES), 1)
    total = jnp.where(lane % 128 >= 120, jnp.sum(rows_ref[...], axis=0), 0.0)
    for k in range(peers):
        out_ref[k] = out[k * each:(k + 1) * each] + total


PARAMS = pltpu.CompilerParams(vmem_limit_bytes=48 * 1024 * 1024)


def shaped(*shape):
    return jax.ShapeDtypeStruct(shape, F32)


def call(kernel, out_shape, name, scratch=()):
    return pl.pallas_call(
        kernel, out_shape=out_shape, scratch_shapes=list(scratch), compiler_params=PARAMS, name=name
    )


def local(state_field, cotangent, spec_weight, point_weight, bias_vector):
    peers = lax.axis_size("gx")
    owned = spec_weight.shape[0]
    full_x = state_field.shape[0] * peers
    norm_scale = float(full_x * NY * ZT) ** (-0.5)
    plain = depth_time(full_x, peers, False)
    double = depth_time(full_x, peers, True)
    y_table = y_tables()
    x_lift, x_modes, x_lower = x_tables(full_x, owned)
    place, spot = small_tables()

    rows_all = 2 * MZT
    width = owned * 24
    block = MY * MX * 2 * C
    field = state_field.reshape(CY, ZT)
    cot = cotangent.reshape(CY, ZT)
    weight = spec_weight.transpose(0, 1, 2, 4, 3, 5).reshape(owned * block, C)
    eye = jnp.eye(NY, dtype=F32)
    mix_in = jnp.einsum("oi,yz->iyoz", point_weight, eye, precision=lax.Precision.HIGHEST).reshape(CY, CY)
    mix_out = jnp.einsum("io,yz->iyoz", point_weight, eye, precision=lax.Precision.HIGHEST).reshape(CY, CY)
    bias = jnp.repeat(bias_vector, NY).reshape(CY, 1)

    def exchange(rows):
        cut = rows.reshape(peers, 2 * owned, LANES)
        return lax.all_to_all(cut, "gx", split_axis=0, concat_axis=0, tiled=True)

    weight_spec = pl.BlockSpec((block, C), lambda m: (m, 0))
    ab_spec = pl.BlockSpec((1, MY * 40, 128), lambda m: (m, 0, 0))
    modes_spec = pl.BlockSpec((1, MY, 24, C), lambda m: (m, 0, 0, 0))
    scratch = [pltpu.VMEM((LANES, width), F32)] * 2

    sent = call(lift_kernel, shaped(rows_all, LANES), "lift")(field, plain, y_table)
    got = exchange(sent).reshape(rows_all, LANES)
    ab = call(functools.partial(gather_kernel, owned), shaped(owned, MY * 40, 128), "x_modes", scratch)(got, x_lift)
    mixed = pl.pallas_call(
        mix_kernel, grid=(owned,), in_specs=[weight_spec, ab_spec], out_specs=modes_spec,
        out_shape=shaped(owned, MY, 24, C), compiler_params=PARAMS, name="mix",
    )(weight, ab)
    sent = call(
        functools.partial(spread_kernel, owned), shaped(rows_all, LANES), "x_rows",
        [pltpu.VMEM((width, LANES), F32)],
    )(mixed, x_lower)
    got = exchange(sent).reshape(rows_all, LANES)
    layer_out, dpre, sent = call(
        middle_kernel, (shaped(CY, ZT), shaped(CY, ZT), shaped(rows_all, LANES)), "middle"
    )(got, field, cot, mix_in, bias, double, y_table, place, spot)
    got = exchange(sent)
    back = call(
        functools.partial(back_modes_kernel, owned), shaped(owned, MY, 24, C), "back_modes"
    )(got.reshape(rows_all, LANES), x_modes)
    grad, sums = pl.pallas_call(
        grad_kernel, grid=(owned,), in_specs=[weight_spec, ab_spec, modes_spec],
        out_specs=(weight_spec, ab_spec),
        out_shape=(shaped(owned * block, C), shaped(owned, MY * 40, 128)),
        compiler_params=PARAMS, name="grads",
    )(weight, ab, back)
    sent = call(
        functools.partial(back_spread_kernel, owned), shaped(peers, 2 * owned, LANES), "back_rows", scratch
    )(sums, x_lower, got)
    got = exchange(sent).reshape(rows_all, LANES)
    field_grad = call(last_kernel, shaped(CY, ZT), "last")(got, dpre, mix_out, plain, y_table)
    small = got[:2 * C].reshape(C, 2, 2, 128)[..., 120:].reshape(C, 32) * norm_scale
    spec_grad = grad.reshape(owned, MY, MX, C, 2, C).transpose(0, 1, 2, 4, 3, 5)
    return (
        layer_out.reshape(state_field.shape),
        field_grad.reshape(state_field.shape),
        spec_grad,
        small[:, :C].T,
        small[:, C],
    )


def solution(mesh):
    in_specs = (
        P(("grp", "gx"), None, None, None),
        P(("grp", "gx"), None, None, None),
        P("gx", None, None, None, None, None),
        P(),
        P(),
    )
    out_specs = (
        P(("grp", "gx"), None, None, None),
        P(("grp", "gx"), None, None, None),
        P(("grp", "gx"), None, None, None, None, None),
        P("grp", None),
        P("grp"),
    )
    return jax.shard_map(local, mesh=mesh, in_specs=in_specs, out_specs=out_specs, check_vma=False)
```

```python
import functools
import math

import jax
import jax.numpy as jnp
import numpy as np
from jax import lax
from jax.experimental import pallas as pl
from jax.experimental.pallas import tpu as pltpu
from jax.sharding import PartitionSpec as P

C = 20
MX = 12
MY = 12
MZ = 24
MT = 8
NZ = 32
NT = 16
NY = 16
ZT = NZ * NT
MZT = MZ * MT
CY = C * NY
HALF = MY // 2
LANES = 256
BF = jnp.bfloat16
F32 = jnp.float32
NN = ((1,), (0,))
NT_DIMS = ((1,), (1,))


def column(ky):
    return (ky // HALF) * 128 + (ky % HALF) * C


def freqs(count):
    modes = np.arange(count)
    return np.where(modes < count // 2, modes, modes - count)


def angles(count, length):
    phase = np.mod(freqs(count)[:, None] * np.arange(length)[None, :], length)
    return 2.0 * np.pi / length * phase


def halves(table):
    table = np.asarray(table, np.float64)
    high = table.astype(jnp.bfloat16)
    low = (table - high.astype(np.float64)).astype(jnp.bfloat16)
    return np.stack([high, low])


def depth_time(full_x, owners, doubled):
    scale = float(full_x * NY * ZT) ** (-0.5)
    modes = np.arange(MZT)
    depth = freqs(MZ)[modes // MT]
    time = modes % MT
    cells = np.arange(ZT)
    phase = depth[:, None] * (cells // NT)[None, :] * NT + time[:, None] * (cells % NT)[None, :] * NZ
    angle = 2.0 * np.pi / ZT * np.mod(phase, ZT)
    factor = np.full((MZT, 1), scale)
    if doubled:
        factor = factor * np.where(time == 0, 1.0, 2.0)[:, None]
    real, imag = factor * np.cos(angle), -factor * np.sin(angle)

    def rows(first, second):
        both = np.stack([first, second]).reshape(2, owners, MZT // owners, ZT)
        return both.transpose(1, 0, 2, 3).reshape(2 * MZT, ZT)

    return halves(np.stack([rows(real, imag), rows(imag, -real)]))


def y_tables():
    angle = angles(MY, NY)
    out = np.zeros((2, C, NY, LANES))
    for ky in range(MY):
        for c in range(C):
            out[0, c, :, column(ky) + c] = np.cos(angle[ky])
            out[1, c, :, column(ky) + c] = np.sin(angle[ky])
    return halves(out.reshape(2, CY, LANES))


def x_tables(full_x, owned):
    angle = angles(MX, full_x)
    cos, sin = np.cos(angle), np.sin(angle)
    eye = np.eye(owned)
    to_real = np.stack([cos, sin])
    to_imag = np.stack([-sin, cos])

    def lift(pair):
        grown = np.einsum("tpkx,mn->xpmntk", pair, eye)
        return grown.reshape(full_x * 2 * owned, owned * 2 * MX)

    even = lift(np.stack([to_real, to_imag]))
    odd = lift(np.stack([-to_imag, to_real]))
    modes = even.T
    from_real = np.stack([cos, sin])
    from_imag = np.stack([-sin, cos])
    lower = lift(np.stack([from_real, from_imag]))
    lower_odd = lift(np.stack([-from_imag, from_real]))
    return halves(np.stack([even, odd])), halves(modes), halves(np.stack([lower, lower_odd]))


def small_tables():
    place = np.zeros((2, C, NY, LANES))
    for i in range(C):
        j = i % 16
        place[i // 16, i, :, (j // 8) * 128 + 120 + j % 8] = 1.0
    spot = np.zeros((2, 2 * MZT, C, NY))
    for o in range(C):
        spot[0, 2 * o, o] = 1.0
        spot[1, 2 * o + 1, o] = 1.0
    return (
        place.reshape(2, CY, LANES).astype(jnp.bfloat16),
        spot.reshape(2, 2 * MZT, CY).astype(jnp.bfloat16),
    )


def split(value):
    high = value.astype(BF)
    return high, (value - high.astype(F32)).astype(BF)


def product(left, right, dims):
    def one(a, b):
        return lax.dot_general(a, b, (dims, ((), ())), preferred_element_type=F32)

    return one(left[0], right[0]) + (one(left[0], right[1]) + one(left[1], right[0]))


def table(ref, *index):
    return ref[(0,) + index], ref[(1,) + index]


def to_rows(field, depth_ref, y_ref):
    out = None
    for k in range(2):
        lifted = product(table(depth_ref, k), field, NT_DIMS)
        term = product(split(lifted), table(y_ref, k), NN)
        out = term if out is None else out + term
    return out


def to_cells(rows, depth_ref, y_ref):
    out = None
    for k in range(2):
        spread = product(table(y_ref, k), rows, NT_DIMS)
        term = product(split(spread), table(depth_ref, k), NN)
        out = term if out is None else out + term
    return out


def lift_kernel(field_ref, depth_ref, y_ref, out_ref):
    out_ref[...] = to_rows(split(field_ref[...]), depth_ref, y_ref)


def middle_kernel(
    rows_ref, field_ref, cot_ref, mix_ref, bias_ref, depth_ref, y_ref, place_ref, spot_ref,
    out_ref, dpre_ref, send_ref,
):
    field = split(field_ref[...])
    pre = to_cells(split(rows_ref[...]), depth_ref, y_ref)
    pre = pre + product(split(mix_ref[...]), field, NN) + bias_ref[...]
    cumulative = 0.5 * (1.0 + lax.erf(pre * (1.0 / math.sqrt(2.0))))
    density = jnp.exp(-0.5 * pre * pre) * (1.0 / math.sqrt(2.0 * math.pi))
    out_ref[...] = pre * cumulative
    dpre = cot_ref[...] * (cumulative + pre * density)
    dpre_ref[...] = dpre
    parts = split(dpre)
    send = to_rows(parts, depth_ref, y_ref)
    cross = product(parts, field, NT_DIMS)
    row = lax.broadcasted_iota(jnp.int32, (CY, CY), 0)
    col = lax.broadcasted_iota(jnp.int32, (CY, CY), 1)
    cross = split(jnp.where((row % NY) == (col % NY), cross, 0.0))
    lane = lax.broadcasted_iota(jnp.int32, (CY, LANES), 1)
    total = jnp.sum(dpre, axis=1, keepdims=True)
    for k in range(2):
        moved = jnp.dot(cross[0], place_ref[k], preferred_element_type=F32)
        moved = moved + jnp.dot(cross[1], place_ref[k], preferred_element_type=F32)
        if k == 1:
            moved = moved + jnp.where(lane == 124, total, 0.0)
        high, low = split(moved)
        send = send + jnp.dot(spot_ref[k], high, preferred_element_type=F32)
        send = send + jnp.dot(spot_ref[k], low, preferred_element_type=F32)
    send_ref[...] = send


def last_kernel(rows_ref, dpre_ref, mix_ref, depth_ref, y_ref, out_ref):
    grad = to_cells(split(rows_ref[...]), depth_ref, y_ref)
    out_ref[...] = grad + product(split(mix_ref[...]), split(dpre_ref[...]), NN)


def gather_kernel(owned, rows_ref, x_ref, ab_ref, even_ref, odd_ref):
    turned = split(rows_ref[...].T)
    even_ref[...] = product(turned, table(x_ref, 0), NN)
    odd_ref[...] = product(turned, table(x_ref, 1), NN)
    for m in range(owned):
        for p, ref in enumerate((even_ref, odd_ref)):
            part = ref[:, m * 24:(m + 1) * 24]
            part = jnp.concatenate([part, part, part, jnp.zeros((LANES, 56), F32)], axis=1)
            for ky in range(MY):
                ab_ref[m, pl.ds(ky * 40 + p, C, stride=2), :] = part[column(ky):column(ky) + C]


def pieces(ab):
    high = ab.astype(BF).astype(F32)
    lane = lax.broadcasted_iota(jnp.int32, ab.shape, 1)
    return jnp.where((lane >= 24) & (lane < 48), ab - high, high)


def stacked(value, order):
    high = value.astype(BF).astype(F32)
    parts = {"h": high, "l": value - high}
    return jnp.concatenate([parts[k] for k in order], axis=0)


def mix_kernel(weight_ref, ab_ref, tile_ref, out_ref):
    row = lax.broadcasted_iota(jnp.int32, (48, 480), 0)
    lane = lax.broadcasted_iota(jnp.int32, (48, 480), 1)
    own = (row % MX) == (lane // 40)
    for ky in range(MY):
        ab = pieces(ab_ref[0, ky * 40:(ky + 1) * 40, :]).T[:48].astype(BF)
        wide = jnp.dot(ab, tile_ref[...], preferred_element_type=F32)
        wide = jnp.where(own, wide, 0.0).astype(BF)
        high, low = split(weight_ref[ky * 480:(ky + 1) * 480, :])
        out = jnp.dot(wide, high, preferred_element_type=F32)
        out = out + jnp.dot(wide, low, preferred_element_type=F32)
        out_ref[0, ky] = out[:24] + out[24:]


def spread_kernel(owned, modes_ref, x_ref, out_ref, full_ref):
    full_ref[...] = jnp.zeros_like(full_ref)
    for ky in range(MY):
        part = modes_ref[:, ky].reshape(owned * 24, C)
        full_ref[:, column(ky):column(ky) + C] = part
    out_ref[...] = product(table(x_ref, 0), split(full_ref[...]), NN)


def back_modes_kernel(owned, rows_ref, x_ref, out_ref):
    modes = product(table(x_ref), split(rows_ref[...]), NN)
    for ky in range(MY):
        part = modes[:, column(ky):column(ky) + C]
        out_ref[:, ky] = part.reshape(owned, 24, C)


def grad_kernel(weight_ref, ab_ref, back_ref, grad_ref, sums_ref):
    lane = lax.broadcasted_iota(jnp.int32, (480, 128), 1)
    row = lax.broadcasted_iota(jnp.int32, (480, 128), 0)
    own = (lane % MX) == (row // 40)
    own_sums = own[:, :48]
    for ky in range(MY):
        ab = pieces(ab_ref[0, ky * 40:(ky + 1) * 40, :])
        wide = jnp.where(own, jnp.concatenate([ab] * MX, axis=0), 0.0).astype(BF)
        back = back_ref[0, ky]
        deep = jnp.concatenate([stacked(back, "hhl"), jnp.zeros((56, C), F32)], axis=0).astype(BF)
        grad_ref[ky * 480:(ky + 1) * 480, :] = jnp.dot(wide, deep, preferred_element_type=F32)
        across = stacked(back, "hl").astype(BF)
        high, low = split(weight_ref[ky * 480:(ky + 1) * 480, :])
        sums = lax.dot_general(high, across, (NT_DIMS, ((), ())), preferred_element_type=F32)
        sums = sums + lax.dot_general(low, across, (NT_DIMS, ((), ())), preferred_element_type=F32)
        sums = jnp.where(own_sums, sums, 0.0)
        total = sums[:40]
        for kx in range(1, MX):
            total = total + sums[kx * 40:(kx + 1) * 40]
        sums_ref[0, ky * 40:(ky + 1) * 40, 0:48] = total


def back_spread_kernel(owned, sums_ref, x_ref, rows_ref, out_ref, even_ref, odd_ref):
    even_ref[...] = jnp.zeros_like(even_ref)
    odd_ref[...] = jnp.zeros_like(odd_ref)
    for m in range(owned):
        for p, ref in enumerate((even_ref, odd_ref)):
            for ky in range(MY):
                part = sums_ref[m, pl.ds(ky * 40 + p, C, stride=2), :]
                part = part[:, :24] + part[:, 24:48]
                ref[column(ky):column(ky) + C, m * 24:(m + 1) * 24] = part
    out = product(table(x_ref, 0), split(even_ref[...]), NT_DIMS)
    out = out + product(table(x_ref, 1), split(odd_ref[...]), NT_DIMS)
    peers, each, _ = rows_ref.shape
    lane = lax.broadcasted_iota(jnp.int32, (each, LANES), 1)
    total = jnp.where(lane % 128 >= 120, jnp.sum(rows_ref[...], axis=0), 0.0)
    for k in range(peers):
        out_ref[k] = out[k * each:(k + 1) * each] + total


PARAMS = pltpu.CompilerParams(vmem_limit_bytes=48 * 1024 * 1024)


def shaped(*shape):
    return jax.ShapeDtypeStruct(shape, F32)


def call(kernel, out_shape, name, scratch=()):
    return pl.pallas_call(
        kernel, out_shape=out_shape, scratch_shapes=list(scratch), compiler_params=PARAMS, name=name
    )


def local(state_field, cotangent, spec_weight, point_weight, bias_vector):
    peers = lax.axis_size("gx")
    owned = spec_weight.shape[0]
    full_x = state_field.shape[0] * peers
    norm_scale = float(full_x * NY * ZT) ** (-0.5)
    plain = depth_time(full_x, peers, False)
    double = depth_time(full_x, peers, True)
    y_table = y_tables()
    x_lift, x_modes, x_lower = x_tables(full_x, owned)
    place, spot = small_tables()

    rows_all = 2 * MZT
    width = owned * 24
    block = MY * MX * 2 * C
    field = state_field.reshape(CY, ZT)
    cot = cotangent.reshape(CY, ZT)
    weight = spec_weight.transpose(0, 1, 2, 4, 3, 5).reshape(owned * block, C)
    eye = jnp.eye(NY, dtype=F32)
    mix_in = jnp.einsum("oi,yz->iyoz", point_weight, eye, precision=lax.Precision.HIGHEST).reshape(CY, CY)
    mix_out = jnp.einsum("io,yz->iyoz", point_weight, eye, precision=lax.Precision.HIGHEST).reshape(CY, CY)
    bias = jnp.repeat(bias_vector, NY).reshape(CY, 1)

    def exchange(rows):
        cut = rows.reshape(peers, 2 * owned, LANES)
        return lax.all_to_all(cut, "gx", split_axis=0, concat_axis=0, tiled=True)

    weight_spec = pl.BlockSpec((block, C), lambda m: (m, 0))
    ab_spec = pl.BlockSpec((1, MY * 40, 128), lambda m: (m, 0, 0))
    tiling = np.tile(np.eye(2 * C), (1, MX)).astype(jnp.bfloat16)
    tile_spec = pl.BlockSpec((2 * C, 2 * C * MX), lambda m: (0, 0))
    modes_spec = pl.BlockSpec((1, MY, 24, C), lambda m: (m, 0, 0, 0))
    scratch = [pltpu.VMEM((LANES, width), F32)] * 2

    sent = call(lift_kernel, shaped(rows_all, LANES), "lift")(field, plain, y_table)
    got = exchange(sent).reshape(rows_all, LANES)
    ab = call(functools.partial(gather_kernel, owned), shaped(owned, MY * 40, 128), "x_modes", scratch)(got, x_lift)
    mixed = pl.pallas_call(
        mix_kernel, grid=(owned,), in_specs=[weight_spec, ab_spec, tile_spec], out_specs=modes_spec,
        out_shape=shaped(owned, MY, 24, C), compiler_params=PARAMS, name="mix",
    )(weight, ab, tiling)
    sent = call(
        functools.partial(spread_kernel, owned), shaped(rows_all, LANES), "x_rows",
        [pltpu.VMEM((width, LANES), F32)],
    )(mixed, x_lower)
    got = exchange(sent).reshape(rows_all, LANES)
    layer_out, dpre, sent = call(
        middle_kernel, (shaped(CY, ZT), shaped(CY, ZT), shaped(rows_all, LANES)), "middle"
    )(got, field, cot, mix_in, bias, double, y_table, place, spot)
    got = exchange(sent)
    back = call(
        functools.partial(back_modes_kernel, owned), shaped(owned, MY, 24, C), "back_modes"
    )(got.reshape(rows_all, LANES), x_modes)
    grad, sums = pl.pallas_call(
        grad_kernel, grid=(owned,), in_specs=[weight_spec, ab_spec, modes_spec],
        out_specs=(weight_spec, ab_spec),
        out_shape=(shaped(owned * block, C), shaped(owned, MY * 40, 128)),
        compiler_params=PARAMS, name="grads",
    )(weight, ab, back)
    sent = call(
        functools.partial(back_spread_kernel, owned), shaped(peers, 2 * owned, LANES), "back_rows", scratch
    )(sums, x_lower, got)
    got = exchange(sent).reshape(rows_all, LANES)
    field_grad = call(last_kernel, shaped(CY, ZT), "last")(got, dpre, mix_out, plain, y_table)
    small = got[:2 * C].reshape(C, 2, 2, 128)[..., 120:].reshape(C, 32) * norm_scale
    spec_grad = grad.reshape(owned, MY, MX, C, 2, C).transpose(0, 1, 2, 4, 3, 5)
    return (
        layer_out.reshape(state_field.shape),
        field_grad.reshape(state_field.shape),
        spec_grad,
        small[:, :C].T,
        small[:, C],
    )


def solution(mesh):
    in_specs = (
        P(("grp", "gx"), None, None, None),
        P(("grp", "gx"), None, None, None),
        P("gx", None, None, None, None, None),
        P(),
        P(),
    )
    out_specs = (
        P(("grp", "gx"), None, None, None),
        P(("grp", "gx"), None, None, None),
        P(("grp", "gx"), None, None, None, None, None),
        P("grp", None),
        P("grp"),
    )
    return jax.shard_map(local, mesh=mesh, in_specs=in_specs, out_specs=out_specs, check_vma=False)
```

```python
import functools
import math

import jax
import jax.numpy as jnp
import numpy as np
from jax import lax
from jax.experimental import pallas as pl
from jax.experimental.pallas import tpu as pltpu
from jax.sharding import PartitionSpec as P

C = 20
MX = 12
MY = 12
MZ = 24
MT = 8
NZ = 32
NT = 16
NY = 16
ZT = NZ * NT
MZT = MZ * MT
CY = C * NY
HALF = MY // 2
LANES = 256
BF = jnp.bfloat16
F32 = jnp.float32
NN = ((1,), (0,))
NT_DIMS = ((1,), (1,))


def column(ky):
    return (ky // HALF) * 128 + (ky % HALF) * C


def freqs(count):
    modes = np.arange(count)
    return np.where(modes < count // 2, modes, modes - count)


def angles(count, length):
    phase = np.mod(freqs(count)[:, None] * np.arange(length)[None, :], length)
    return 2.0 * np.pi / length * phase


def halves(table):
    table = np.asarray(table, np.float64)
    high = table.astype(jnp.bfloat16)
    low = (table - high.astype(np.float64)).astype(jnp.bfloat16)
    return np.stack([high, low])


def depth_time(full_x, owners, doubled):
    scale = float(full_x * NY * ZT) ** (-0.5)
    modes = np.arange(MZT)
    depth = freqs(MZ)[modes // MT]
    time = modes % MT
    cells = np.arange(ZT)
    phase = depth[:, None] * (cells // NT)[None, :] * NT + time[:, None] * (cells % NT)[None, :] * NZ
    angle = 2.0 * np.pi / ZT * np.mod(phase, ZT)
    factor = np.full((MZT, 1), scale)
    if doubled:
        factor = factor * np.where(time == 0, 1.0, 2.0)[:, None]
    real, imag = factor * np.cos(angle), -factor * np.sin(angle)

    def rows(first, second):
        both = np.stack([first, second]).reshape(2, owners, MZT // owners, ZT)
        return both.transpose(1, 0, 2, 3).reshape(2 * MZT, ZT)

    return halves(np.stack([rows(real, imag), rows(imag, -real)]))


def y_tables():
    angle = angles(MY, NY)
    out = np.zeros((2, C, NY, LANES))
    for ky in range(MY):
        for c in range(C):
            out[0, c, :, column(ky) + c] = np.cos(angle[ky])
            out[1, c, :, column(ky) + c] = np.sin(angle[ky])
    return halves(out.reshape(2, CY, LANES))


def x_tables(full_x, owned):
    angle = angles(MX, full_x)
    cos, sin = np.cos(angle), np.sin(angle)
    eye = np.eye(owned)
    to_real = np.stack([cos, sin])
    to_imag = np.stack([-sin, cos])

    def lift(pair):
        grown = np.einsum("tpkx,mn->xpmntk", pair, eye)
        return grown.reshape(full_x * 2 * owned, owned * 2 * MX)

    even = lift(np.stack([to_real, to_imag]))
    odd = lift(np.stack([-to_imag, to_real]))
    modes = even.T
    from_real = np.stack([cos, sin])
    from_imag = np.stack([-sin, cos])
    lower = lift(np.stack([from_real, from_imag]))
    lower_odd = lift(np.stack([-from_imag, from_real]))
    return halves(np.stack([even, odd])), halves(modes), halves(np.stack([lower, lower_odd]))


def small_tables():
    place = np.zeros((2, C, NY, LANES))
    for i in range(C):
        j = i % 16
        place[i // 16, i, :, (j // 8) * 128 + 120 + j % 8] = 1.0
    spot = np.zeros((2, 2 * MZT, C, NY))
    for o in range(C):
        spot[0, 2 * o, o] = 1.0
        spot[1, 2 * o + 1, o] = 1.0
    return (
        place.reshape(2, CY, LANES).astype(jnp.bfloat16),
        spot.reshape(2, 2 * MZT, CY).astype(jnp.bfloat16),
    )


def split(value):
    high = value.astype(BF)
    return high, (value - high.astype(F32)).astype(BF)


def product(left, right, dims):
    def one(a, b):
        return lax.dot_general(a, b, (dims, ((), ())), preferred_element_type=F32)

    return one(left[0], right[0]) + (one(left[0], right[1]) + one(left[1], right[0]))


def table(ref, *index):
    return ref[(0,) + index], ref[(1,) + index]


def to_rows(field, depth_ref, y_ref):
    out = None
    for k in range(2):
        lifted = product(table(depth_ref, k), field, NT_DIMS)
        term = product(split(lifted), table(y_ref, k), NN)
        out = term if out is None else out + term
    return out


def to_cells(rows, depth_ref, y_ref):
    out = None
    for k in range(2):
        spread = product(table(y_ref, k), rows, NT_DIMS)
        term = product(split(spread), table(depth_ref, k), NN)
        out = term if out is None else out + term
    return out


def pointwise(weight_ref, repeat_ref, dims):
    row = lax.broadcasted_iota(jnp.int32, (CY, CY), 0)
    lane = lax.broadcasted_iota(jnp.int32, (CY, CY), 1)
    repeat = repeat_ref[...]

    def one(part):
        tall = lax.dot_general(repeat, part, (dims, ((), ())), preferred_element_type=F32).astype(BF)
        full = lax.dot_general(tall, repeat, (NT_DIMS, ((), ())), preferred_element_type=F32)
        return jnp.where((row % NY) == (lane % NY), full, 0.0).astype(BF)

    high, low = split(weight_ref[...])
    return one(high), one(low)


def exchange_kernel(rows_ref, out_ref, send_sem, recv_sem, own_sem):
    peers = rows_ref.shape[0]
    me = lax.axis_index("gx")
    barrier = pltpu.get_barrier_semaphore()

    def greet(k, carry):
        pl.semaphore_signal(
            barrier, inc=1, device_id={"gx": lax.rem(me + k, peers)},
            device_id_type=pl.DeviceIdType.MESH,
        )
        return carry

    def moved(k):
        peer = lax.rem(me + k, peers)
        return pltpu.make_async_remote_copy(
            src_ref=rows_ref.at[peer], dst_ref=out_ref.at[me], send_sem=send_sem.at[k],
            recv_sem=recv_sem.at[k], device_id={"gx": peer}, device_id_type=pl.DeviceIdType.MESH,
        )

    def begin(k, carry):
        moved(k).start()
        return carry

    def finish(k, carry):
        moved(k).wait()
        return carry

    lax.fori_loop(1, peers, greet, 0)
    own = pltpu.make_async_copy(rows_ref.at[me], out_ref.at[me], own_sem)
    own.start()
    pl.semaphore_wait(barrier, peers - 1)
    lax.fori_loop(1, peers, begin, 0)
    own.wait()
    lax.fori_loop(1, peers, finish, 0)


def lift_kernel(field_ref, depth_ref, y_ref, out_ref):
    out_ref[...] = to_rows(split(field_ref[...]), depth_ref, y_ref)


def middle_kernel(
    rows_ref, field_ref, cot_ref, mix_ref, repeat_ref, bias_ref, depth_ref, y_ref, place_ref, spot_ref,
    out_ref, dpre_ref, send_ref,
):
    field = split(field_ref[...])
    pre = to_cells(split(rows_ref[...]), depth_ref, y_ref)
    pre = pre + product(pointwise(mix_ref, repeat_ref, NT_DIMS), field, NN) + bias_ref[...]
    cumulative = 0.5 * (1.0 + lax.erf(pre * (1.0 / math.sqrt(2.0))))
    density = jnp.exp(-0.5 * pre * pre) * (1.0 / math.sqrt(2.0 * math.pi))
    out_ref[...] = pre * cumulative
    dpre = cot_ref[...] * (cumulative + pre * density)
    dpre_ref[...] = dpre
    parts = split(dpre)
    send = to_rows(parts, depth_ref, y_ref)
    cross = product(parts, field, NT_DIMS)
    row = lax.broadcasted_iota(jnp.int32, (CY, CY), 0)
    col = lax.broadcasted_iota(jnp.int32, (CY, CY), 1)
    cross = split(jnp.where((row % NY) == (col % NY), cross, 0.0))
    lane = lax.broadcasted_iota(jnp.int32, (CY, LANES), 1)
    total = jnp.sum(dpre, axis=1, keepdims=True)
    for k in range(2):
        moved = jnp.dot(cross[0], place_ref[k], preferred_element_type=F32)
        moved = moved + jnp.dot(cross[1], place_ref[k], preferred_element_type=F32)
        if k == 1:
            moved = moved + jnp.where(lane == 124, total, 0.0)
        high, low = split(moved)
        send = send + jnp.dot(spot_ref[k], high, preferred_element_type=F32)
        send = send + jnp.dot(spot_ref[k], low, preferred_element_type=F32)
    send_ref[...] = send


def last_kernel(rows_ref, dpre_ref, mix_ref, repeat_ref, depth_ref, y_ref, out_ref):
    grad = to_cells(split(rows_ref[...]), depth_ref, y_ref)
    out_ref[...] = grad + product(pointwise(mix_ref, repeat_ref, NN), split(dpre_ref[...]), NN)


def gather_kernel(owned, rows_ref, x_ref, ab_ref, even_ref, odd_ref):
    turned = split(rows_ref[...].T)
    even_ref[...] = product(turned, table(x_ref, 0), NN)
    odd_ref[...] = product(turned, table(x_ref, 1), NN)
    for m in range(owned):
        for p, ref in enumerate((even_ref, odd_ref)):
            part = ref[:, m * 24:(m + 1) * 24]
            part = jnp.concatenate([part, part, part, jnp.zeros((LANES, 56), F32)], axis=1)
            for ky in range(MY):
                ab_ref[m, pl.ds(ky * 40 + p, C, stride=2), :] = part[column(ky):column(ky) + C]


def pieces(ab):
    high = ab.astype(BF).astype(F32)
    lane = lax.broadcasted_iota(jnp.int32, ab.shape, 1)
    return jnp.where((lane >= 24) & (lane < 48), ab - high, high)


def stacked(value, order):
    high = value.astype(BF).astype(F32)
    parts = {"h": high, "l": value - high}
    return jnp.concatenate([parts[k] for k in order], axis=0)


def mix_kernel(weight_ref, ab_ref, tile_ref, out_ref):
    row = lax.broadcasted_iota(jnp.int32, (48, 480), 0)
    lane = lax.broadcasted_iota(jnp.int32, (48, 480), 1)
    own = (row % MX) == (lane // 40)
    for ky in range(MY):
        ab = pieces(ab_ref[0, ky * 40:(ky + 1) * 40, :]).T[:48].astype(BF)
        wide = jnp.dot(ab, tile_ref[...], preferred_element_type=F32)
        wide = jnp.where(own, wide, 0.0).astype(BF)
        high, low = split(weight_ref[ky * 480:(ky + 1) * 480, :])
        out = jnp.dot(wide, high, preferred_element_type=F32)
        out = out + jnp.dot(wide, low, preferred_element_type=F32)
        out_ref[0, ky] = out[:24] + out[24:]


def spread_kernel(owned, modes_ref, x_ref, out_ref, full_ref):
    full_ref[...] = jnp.zeros_like(full_ref)
    for ky in range(MY):
        part = modes_ref[:, ky].reshape(owned * 24, C)
        full_ref[:, column(ky):column(ky) + C] = part
    out_ref[...] = product(table(x_ref, 0), split(full_ref[...]), NN)


def back_modes_kernel(owned, rows_ref, x_ref, out_ref):
    modes = product(table(x_ref), split(rows_ref[...]), NN)
    for ky in range(MY):
        part = modes[:, column(ky):column(ky) + C]
        out_ref[:, ky] = part.reshape(owned, 24, C)


def grad_kernel(weight_ref, ab_ref, back_ref, grad_ref, sums_ref):
    lane = lax.broadcasted_iota(jnp.int32, (480, 128), 1)
    row = lax.broadcasted_iota(jnp.int32, (480, 128), 0)
    own = (lane % MX) == (row // 40)
    own_sums = own[:, :48]
    for ky in range(MY):
        ab = pieces(ab_ref[0, ky * 40:(ky + 1) * 40, :])
        wide = jnp.where(own, jnp.concatenate([ab] * MX, axis=0), 0.0).astype(BF)
        back = back_ref[0, ky]
        deep = jnp.concatenate([stacked(back, "hhl"), jnp.zeros((56, C), F32)], axis=0).astype(BF)
        grad_ref[ky * 480:(ky + 1) * 480, :] = jnp.dot(wide, deep, preferred_element_type=F32)
        across = stacked(back, "hl").astype(BF)
        high, low = split(weight_ref[ky * 480:(ky + 1) * 480, :])
        sums = lax.dot_general(high, across, (NT_DIMS, ((), ())), preferred_element_type=F32)
        sums = sums + lax.dot_general(low, across, (NT_DIMS, ((), ())), preferred_element_type=F32)
        sums = jnp.where(own_sums, sums, 0.0)
        total = sums[:40]
        for kx in range(1, MX):
            total = total + sums[kx * 40:(kx + 1) * 40]
        sums_ref[0, ky * 40:(ky + 1) * 40, 0:24] = total[:, :24] + total[:, 24:]


def back_spread_kernel(owned, sums_ref, x_ref, rows_ref, out_ref, even_ref, odd_ref):
    even_ref[...] = jnp.zeros_like(even_ref)
    odd_ref[...] = jnp.zeros_like(odd_ref)
    for m in range(owned):
        for p, ref in enumerate((even_ref, odd_ref)):
            for ky in range(MY):
                part = sums_ref[m, pl.ds(ky * 40 + p, C, stride=2), :]
                ref[column(ky):column(ky) + C, m * 24:(m + 1) * 24] = part[:, :24]
    out = product(table(x_ref, 0), split(even_ref[...]), NT_DIMS)
    out = out + product(table(x_ref, 1), split(odd_ref[...]), NT_DIMS)
    peers, each, _ = rows_ref.shape
    lane = lax.broadcasted_iota(jnp.int32, (each, LANES), 1)
    total = jnp.where(lane % 128 >= 120, jnp.sum(rows_ref[...], axis=0), 0.0)
    for k in range(peers):
        out_ref[k] = out[k * each:(k + 1) * each] + total


PARAMS = pltpu.CompilerParams(vmem_limit_bytes=48 * 1024 * 1024)


def shaped(*shape):
    return jax.ShapeDtypeStruct(shape, F32)


def call(kernel, out_shape, name, scratch=()):
    return pl.pallas_call(
        kernel, out_shape=out_shape, scratch_shapes=list(scratch), compiler_params=PARAMS, name=name
    )


def local(state_field, cotangent, spec_weight, point_weight, bias_vector):
    peers = lax.axis_size("gx")
    owned = spec_weight.shape[0]
    full_x = state_field.shape[0] * peers
    norm_scale = float(full_x * NY * ZT) ** (-0.5)
    plain = depth_time(full_x, peers, False)
    double = depth_time(full_x, peers, True)
    y_table = y_tables()
    x_lift, x_modes, x_lower = x_tables(full_x, owned)
    place, spot = small_tables()

    rows_all = 2 * MZT
    width = owned * 24
    block = MY * MX * 2 * C
    field = state_field.reshape(CY, ZT)
    cot = cotangent.reshape(CY, ZT)
    weight = spec_weight.transpose(0, 1, 2, 4, 3, 5).reshape(owned * block, C)
    repeat = np.repeat(np.eye(C), NY, axis=0).astype(jnp.bfloat16)
    bias = jnp.repeat(bias_vector, NY).reshape(CY, 1)

    def exchange(rows, collective_id):
        cut = rows.reshape(peers, 2 * owned, LANES)
        return pl.pallas_call(
            exchange_kernel,
            out_shape=jax.ShapeDtypeStruct(cut.shape, F32),
            in_specs=[pl.BlockSpec(memory_space=pltpu.VMEM)],
            out_specs=pl.BlockSpec(memory_space=pltpu.VMEM),
            scratch_shapes=[
                pltpu.SemaphoreType.DMA((peers,)), pltpu.SemaphoreType.DMA((peers,)),
                pltpu.SemaphoreType.DMA,
            ],
            compiler_params=pltpu.CompilerParams(collective_id=collective_id, has_side_effects=True),
            name="exchange",
        )(cut)

    weight_spec = pl.BlockSpec((block, C), lambda m: (m, 0))
    ab_spec = pl.BlockSpec((1, MY * 40, 128), lambda m: (m, 0, 0))
    tiling = np.tile(np.eye(2 * C), (1, MX)).astype(jnp.bfloat16)
    tile_spec = pl.BlockSpec((2 * C, 2 * C * MX), lambda m: (0, 0))
    modes_spec = pl.BlockSpec((1, MY, 24, C), lambda m: (m, 0, 0, 0))
    scratch = [pltpu.VMEM((LANES, width), F32)] * 2

    sent = call(lift_kernel, shaped(rows_all, LANES), "lift")(field, plain, y_table)
    got = exchange(sent, 0).reshape(rows_all, LANES)
    ab = call(functools.partial(gather_kernel, owned), shaped(owned, MY * 40, 128), "x_modes", scratch)(got, x_lift)
    mixed = pl.pallas_call(
        mix_kernel, grid=(owned,), in_specs=[weight_spec, ab_spec, tile_spec], out_specs=modes_spec,
        out_shape=shaped(owned, MY, 24, C), compiler_params=PARAMS, name="mix",
    )(weight, ab, tiling)
    sent = call(
        functools.partial(spread_kernel, owned), shaped(rows_all, LANES), "x_rows",
        [pltpu.VMEM((width, LANES), F32)],
    )(mixed, x_lower)
    got = exchange(sent, 1).reshape(rows_all, LANES)
    layer_out, dpre, sent = call(
        middle_kernel, (shaped(CY, ZT), shaped(CY, ZT), shaped(rows_all, LANES)), "middle"
    )(got, field, cot, point_weight, repeat, bias, double, y_table, place, spot)
    got = exchange(sent, 2)
    back = call(
        functools.partial(back_modes_kernel, owned), shaped(owned, MY, 24, C), "back_modes"
    )(got.reshape(rows_all, LANES), x_modes)
    grad, sums = pl.pallas_call(
        grad_kernel, grid=(owned,), in_specs=[weight_spec, ab_spec, modes_spec],
        out_specs=(weight_spec, ab_spec),
        out_shape=(shaped(owned * block, C), shaped(owned, MY * 40, 128)),
        compiler_params=PARAMS, name="grads",
    )(weight, ab, back)
    sent = call(
        functools.partial(back_spread_kernel, owned), shaped(peers, 2 * owned, LANES), "back_rows", scratch
    )(sums, x_lower, got)
    got = exchange(sent, 3).reshape(rows_all, LANES)
    field_grad = call(last_kernel, shaped(CY, ZT), "last")(got, dpre, point_weight, repeat, plain, y_table)
    small = got[:2 * C].reshape(C, 2, 2, 128)[..., 120:].reshape(C, 32) * norm_scale
    spec_grad = grad.reshape(owned, MY, MX, C, 2, C).transpose(0, 1, 2, 4, 3, 5)
    return (
        layer_out.reshape(state_field.shape),
        field_grad.reshape(state_field.shape),
        spec_grad,
        small[:, :C].T,
        small[:, C],
    )


def solution(mesh):
    in_specs = (
        P(("grp", "gx"), None, None, None),
        P(("grp", "gx"), None, None, None),
        P("gx", None, None, None, None, None),
        P(),
        P(),
    )
    out_specs = (
        P(("grp", "gx"), None, None, None),
        P(("grp", "gx"), None, None, None),
        P(("grp", "gx"), None, None, None, None, None),
        P("grp", None),
        P("grp"),
    )
    return jax.shard_map(local, mesh=mesh, in_specs=in_specs, out_specs=out_specs, check_vma=False)
```
